32 devices in a mesh: rep: 4 (over x, core), shard: 8 (over z, y).
Axes of the slice: x: 2, y: 2, z: 4, core: 2. Of those that a mesh axis runs over, the one named last changes fastest.
Arguments:
- conv_input: bfloat16 [32, 256, 6144], P(('rep', 'shard')), may hold values from -24 to 24
- cotangent: bfloat16 [32, 256, 6144], P(('rep', 'shard')), may hold values from -6 to 6
- kernel: bfloat16 [31, 6144], P(None, 'shard'), may hold values from -1 to 1
- conv_bias: bfloat16 [6144], P('shard'), may hold values from -3 to 3
- ln_gain: bfloat16 [6144], P('shard'), may hold values from 0.25 to 1.75
- ln_bias: bfloat16 [6144], P('shard'), may hold values from -3 to 3
Outputs:
- activated: bfloat16 [32, 256, 6144], P(('rep', 'shard'))
- grad_input: bfloat16 [32, 256, 6144], P(('rep', 'shard'))
- grad_kernel: float32 [31, 6144], P(None, 'shard')
- grad_conv_bias: float32 [6144], P('shard')
- grad_gain: float32 [6144], P('shard')
- grad_ln_bias: float32 [6144], P('shard')
The draws below stay inside these ranges and needn't reach their ends.
All inputs are finite; a program needn't handle non-finite values.
Results may differ from the reference program's by a relative error of at most 0.0012.
Values may be sent and summed in bfloat16 or wider, within the bound.
A program may use at most 128 MiB of HBM per device.

```python
import math
import jax
import jax.numpy as jnp
from jax import lax

D = 6144
K = 31
FRAMES = 256
CLIPS = 32


def draw_conv_input(key, part):
    key_chan, key_rows, key_base = jax.random.split(key, 3)
    channel_scale = jnp.exp(jax.random.uniform(key_chan, (D,), jnp.float32, jnp.log(0.2), jnp.log(2.0)))
    row_scale = jnp.exp(jax.random.uniform(key_rows, (CLIPS, FRAMES, 1), jnp.float32, jnp.log(0.3), jnp.log(3.0)))
    base = jax.random.truncated_normal(key_base, -4.0, 4.0, (CLIPS, FRAMES, D), jnp.float32)
    return (base * channel_scale * row_scale).astype(jnp.bfloat16)


def with_spikes(drawn, key, source, target, shards_of, factor):
    def block_of(axis_at):
        return (jnp.arange(drawn.shape[axis_at]) // (drawn.shape[axis_at] // shards_of)).reshape((-1,) + (1,) * (drawn.ndim - 1 - axis_at))

    near = jax.random.permutation(key, shards_of)[block_of(target)]
    far = (block_of(target) + shards_of // 2) % shards_of
    return jnp.where((block_of(source) == near) | (block_of(source) == far), factor * drawn, drawn)


def levels(rng, shape, pieces, smallest, top_value):
    factor_of = 1.0
    for dim, blocks in pieces:
        heights = jax.random.uniform(jax.random.fold_in(jax.random.fold_in(rng, 6), dim), (blocks,), jnp.float32, smallest / len(pieces), top_value / len(pieces))
        factor_of = factor_of * jnp.repeat(jnp.exp(heights), shape[dim] // blocks).reshape((-1,) + (1,) * (len(shape) - 1 - dim))
    return factor_of


def gaussian(key, dims, width, bound, cuts=(), kind=jnp.bfloat16):
    drawn = jax.random.normal(key, dims, jnp.float32) * width
    if len(cuts) > 0:
        drawn = levels(key, dims, cuts, -0.22, 0.18) * drawn
    return jnp.clip(drawn, min=-bound, max=bound).astype(kind)


def bell_draw_with(key, shape, spread, most, shards, heavy, held_as=jnp.bfloat16):
    entries = spread * jax.random.normal(key, shape, jnp.float32)
    if shards:
        entries = entries * levels(key, shape, shards, -0.22, 0.18)
    return jnp.clip(with_spikes(entries, jax.random.fold_in(key, 3), *heavy), -most, most).astype(held_as)


def setup_inputs(seed: int = 0) -> dict:
    keys = jax.random.split(jax.random.key(seed), 7)
    conv_input = draw_conv_input(jax.random.fold_in(keys[6], 71), 0)
    cotangent = bell_draw_with(keys[1], (CLIPS, FRAMES, D), 1.0, 6.0, ((0, 32),), (0, 2, 32, 2.75))
    kernel = gaussian(keys[2], (K, D), K ** -0.5, 1.0, ((1, 8),))
    conv_bias = gaussian(keys[3], (D,), 0.5, 3.0, ((0, 8),))
    ln_gain = jnp.clip(1.0 + 0.15 * jax.random.normal(keys[4], (D,), jnp.float32), 0.25, 1.75).astype(jnp.bfloat16)
    ln_bias = gaussian(keys[5], (D,), 0.5, 3.0, ((0, 8),))
    return {"conv_input": conv_input, "cotangent": cotangent, "kernel": kernel, "conv_bias": conv_bias, "ln_gain": ln_gain, "ln_bias": ln_bias}


def forward_part(frames_in, params):
    taps = params.shape[0] - 3
    half_width = (taps - 1) // 2
    length = frames_in.shape[0]
    padded = jnp.pad(frames_in, ((half_width, half_width), (0, 0)))
    conv_out = params[taps].astype(jnp.float32)[None, :] + params[0].astype(jnp.float32) * padded[0:length].astype(jnp.float32)
    for lag_index in range(1, taps):
        conv_out = conv_out + params[lag_index].astype(jnp.float32) * padded[lag_index:lag_index + length].astype(jnp.float32)
    row_mean = lax.optimization_barrier(jnp.mean(conv_out, axis=-1, keepdims=True))
    centered = conv_out - row_mean
    inverse = lax.rsqrt(lax.optimization_barrier(jnp.mean(centered * centered, axis=-1, keepdims=True)) + 1e-05)
    normed = centered * inverse
    affine = params[taps + 1].astype(jnp.float32) * normed + params[taps + 2].astype(jnp.float32)
    squash = jax.nn.sigmoid(affine)
    activated = (affine * squash).astype(jnp.bfloat16)
    return (activated, normed, inverse, affine, squash)

def backward_part(frames_in, upstream, params, normed, inverse, affine, squash):
    taps = params.shape[0] - 3
    half_width = (taps - 1) // 2
    length = frames_in.shape[0]
    grad_affine = upstream.astype(jnp.float32) * squash * (1.0 + affine * (1.0 - squash))
    grad_normed = grad_affine * params[taps + 1].astype(jnp.float32)
    grad_conv = inverse * (grad_normed - lax.optimization_barrier(jnp.mean(grad_normed, axis=-1, keepdims=True)) - normed * lax.optimization_barrier(jnp.mean(grad_normed * normed, axis=-1, keepdims=True)))
    padded_in = jnp.pad(frames_in, ((half_width, half_width), (0, 0)))
    kernel_rows = [lax.optimization_barrier(jnp.sum(grad_conv * padded_in[lag_index:lag_index + length].astype(jnp.float32), axis=0)) for lag_index in range(taps)]
    padded_grad = jnp.pad(grad_conv, ((half_width, half_width), (0, 0)))
    back_start = 2 * half_width
    grad_input = params[0].astype(jnp.float32) * padded_grad[back_start:back_start + length]
    for lag_index in range(1, taps):
        first = back_start - lag_index
        grad_input = grad_input + params[lag_index].astype(jnp.float32) * padded_grad[first:first + length]
    terms = jnp.concatenate([jnp.stack(kernel_rows, 0), lax.optimization_barrier(jnp.sum(grad_conv, axis=0))[None], lax.optimization_barrier(jnp.sum(grad_affine * normed, axis=0))[None], lax.optimization_barrier(jnp.sum(grad_affine, axis=0))[None]], 0)
    return (grad_input.astype(jnp.bfloat16), terms)

def reference(conv_input, cotangent, kernel, conv_bias, ln_gain, ln_bias):
    params = jnp.concatenate([kernel, conv_bias[None], ln_gain[None], ln_bias[None]], 0)

    def one_clip(running, clip_pair):
        frames_in, upstream = clip_pair
        activated, normed, inverse, affine, squash = forward_part(frames_in, params)
        grad_input, terms = backward_part(frames_in, upstream, params, normed, inverse, affine, squash)
        return (running + terms, (activated, grad_input))
    initial = jnp.zeros((K + 3, D), jnp.float32)
    summed, (activated, grad_input) = lax.scan(one_clip, initial, (conv_input, cotangent))
    grads = summed * (1.0 / math.sqrt(CLIPS * FRAMES))
    return (activated, grad_input, grads[:K], grads[K], grads[K + 1], grads[K + 2])
```

```python
import math

import jax
import jax.numpy as jnp
from jax import lax
from jax.experimental import pallas as pl
from jax.experimental.pallas import tpu as pltpu
from jax.sharding import PartitionSpec as P

LANES = 128
ROWS = 8
PAD = 16
PARAM_ROWS = 48
TERM_ROWS = 40


def lanes_of(index):
    return pl.ds(pl.multiple_of(index * LANES, LANES), LANES)


def shifted_taps(src, base, coef_ref, coef_row, count):
    def by_phase(phase, totals):
        totals = list(totals)
        coefs = [
            jnp.broadcast_to(coef_ref[pl.ds(coef_row(ROWS * a + phase), 1), :], (ROWS, LANES))
            for a in range(4)
        ]
        for m in range(count + 3):
            value = src[pl.ds(base + ROWS * m + phase + 1, ROWS), :]
            for a in range(4):
                if 0 <= m - a < count:
                    totals[m - a] = totals[m - a] + coefs[a] * value
        return tuple(totals)

    return by_phase


def local_kernel(taps, x_ref, cot_ref, par_ref, act_ref, gin_ref, terms_ref,
                 xp, gp, conv, pf, row_a, row_b, row_c, row_d, acc):
    frames, width = x_ref.shape
    count = frames // ROWS
    tiles = width // LANES
    zeros_tile = jnp.zeros((ROWS, LANES), jnp.float32)

    def rows(i):
        return pl.ds(ROWS * i, ROWS)

    long = frames + 2 * PAD
    held = ROWS + PARAM_ROWS

    def at_long(c, start, size):
        return pl.ds(pl.multiple_of(c * long + start, ROWS), size)

    def at_held(c, start, size):
        return pl.ds(c * held + start, size)

    row_a[...] = jnp.zeros_like(row_a)
    row_c[...] = jnp.zeros_like(row_c)
    row_d[...] = jnp.zeros_like(row_d)

    def forward(c, carry):
        lanes = lanes_of(c)
        pf[at_held(c, 0, ROWS), :] = zeros_tile
        pf[at_held(c, ROWS, PARAM_ROWS), :] = par_ref[:, lanes].astype(jnp.float32)
        for ref in (xp, gp):
            for start in (0, PAD + frames):
                ref[at_long(c, start, PAD), :] = jnp.zeros((PAD, LANES), jnp.float32)
        xp[at_long(c, PAD, frames), :] = x_ref[:, lanes].astype(jnp.float32)
        bias = jnp.broadcast_to(pf[at_held(c, ROWS + taps + 1, 1), :], (ROWS, LANES))
        totals = lax.fori_loop(
            0,
            ROWS,
            shifted_taps(xp, c * long, pf, lambda j: c * held + ROWS + j, count),
            (bias,) * count,
        )
        for i in range(count):
            conv[rows(i), lanes] = totals[i]
            row_a[rows(i), :] += totals[i]
        return carry

    lax.fori_loop(0, tiles, forward, 0)

    def stats(i, carry):
        at = pl.ds(pl.multiple_of(i * ROWS, ROWS), ROWS)
        mean = jnp.sum(row_a[at, :], axis=-1, keepdims=True) * (1.0 / width)
        mean = jnp.broadcast_to(mean, (ROWS, LANES))
        parts = [zeros_tile] * 4
        for c in range(tiles):
            off = conv[at, c * LANES : (c + 1) * LANES] - mean
            parts[c % 4] = parts[c % 4] + off * off
        square = (parts[0] + parts[1]) + (parts[2] + parts[3])
        var = jnp.sum(square, axis=-1, keepdims=True) * (1.0 / width)
        row_a[at, :] = mean
        row_b[at, :] = jnp.broadcast_to(lax.rsqrt(var + 1e-05), (ROWS, LANES))
        return carry

    lax.fori_loop(0, count, stats, 0)

    def pointwise(c, carry):
        lanes = lanes_of(c)
        gain = jnp.broadcast_to(pf[at_held(c, ROWS + taps + 2, 1), :], (ROWS, LANES))
        shift = jnp.broadcast_to(pf[at_held(c, ROWS + taps + 3, 1), :], (ROWS, LANES))
        for_gain = [zeros_tile] * 2
        for_bias = [zeros_tile] * 2
        for pair in range(count // 2):
            two = pl.ds(2 * ROWS * pair, 2 * ROWS)
            upstream = cot_ref[two, lanes].astype(jnp.float32)
            acts = []
            for half in range(2):
                i = 2 * pair + half
                normed = (conv[rows(i), lanes] - row_a[rows(i), :]) * row_b[rows(i), :]
                affine = gain * normed + shift
                squash = 0.5 + 0.5 * jnp.tanh(0.5 * affine)
                acts.append(affine * squash)
                up = upstream[half * ROWS : (half + 1) * ROWS]
                grad_affine = up * squash * (1.0 + affine * (1.0 - squash))
                grad_normed = grad_affine * gain
                conv[rows(i), lanes] = normed
                gp[at_long(c, PAD + ROWS * i, ROWS), :] = grad_normed
                row_c[rows(i), :] += grad_normed
                row_d[rows(i), :] += grad_normed * normed
                for_gain[half] = for_gain[half] + grad_affine * normed
                for_bias[half] = for_bias[half] + grad_affine
            act_ref[two, lanes] = jnp.concatenate(acts, 0).astype(jnp.bfloat16)
        terms_ref[32:33, lanes] = jnp.sum(for_gain[0] + for_gain[1], axis=0, keepdims=True)
        terms_ref[33:34, lanes] = jnp.sum(for_bias[0] + for_bias[1], axis=0, keepdims=True)
        return carry

    lax.fori_loop(0, tiles, pointwise, 0)

    def means(i, carry):
        at = pl.ds(pl.multiple_of(i * ROWS, ROWS), ROWS)
        for ref in (row_c, row_d):
            mean = jnp.sum(ref[at, :], axis=-1, keepdims=True) * (1.0 / width)
            ref[at, :] = jnp.broadcast_to(mean, (ROWS, LANES))
        return carry

    lax.fori_loop(0, count, means, 0)

    def weights(c, carry):
        lanes = lanes_of(c)
        grads = []
        total = [zeros_tile] * 2
        for i in range(count):
            grad = row_b[rows(i), :] * (
                gp[at_long(c, PAD + ROWS * i, ROWS), :] - row_c[rows(i), :] - conv[rows(i), lanes] * row_d[rows(i), :]
            )
            gp[at_long(c, PAD + ROWS * i, ROWS), :] = grad
            total[i % 2] = total[i % 2] + grad
            grads.append(grad)

        def by_phase(phase, carry):
            sums = [[zeros_tile, zeros_tile] for _ in range(4)]
            for m in range(count + 3):
                value = xp[pl.ds(c * long + ROWS * m + phase + 1, ROWS), :]
                for a in range(4):
                    if 0 <= m - a < count:
                        sums[a][m % 2] = sums[a][m % 2] + grads[m - a] * value
            for a in range(4):
                start = pl.multiple_of((ROWS * a + phase) * ROWS, ROWS)
                acc[pl.ds(start, ROWS), :] = sums[a][0] + sums[a][1]
            return carry

        lax.fori_loop(0, ROWS, by_phase, 0)
        acc[taps * ROWS : (taps + 1) * ROWS, :] = total[0] + total[1]
        summed = acc[pl.ds(0, 32, stride=ROWS), :]
        for s in range(1, ROWS):
            summed = summed + acc[pl.ds(s, 32, stride=ROWS), :]
        terms_ref[0:32, lanes] = summed
        return carry

    lax.fori_loop(0, tiles, weights, 0)

    def inputs(c, carry):
        lanes = lanes_of(c)
        totals = lax.fori_loop(
            0,
            ROWS,
            shifted_taps(gp, c * long, pf, lambda j: c * held + ROWS + taps - 1 - j, count),
            (zeros_tile,) * count,
        )
        for i in range(count // 2):
            both = jnp.concatenate([totals[2 * i], totals[2 * i + 1]], 0)
            gin_ref[pl.ds(2 * ROWS * i, 2 * ROWS), lanes] = both.astype(jnp.bfloat16)
        return carry

    lax.fori_loop(0, tiles, inputs, 0)


def local_part(frames_in, upstream, params, taps):
    frames, width = frames_in.shape
    vmem = pl.BlockSpec(memory_space=pltpu.VMEM)
    f32 = jnp.float32
    return pl.pallas_call(
        lambda *refs: local_kernel(taps, *refs),
        out_shape=(
            jax.ShapeDtypeStruct((frames, width), jnp.bfloat16),
            jax.ShapeDtypeStruct((frames, width), jnp.bfloat16),
            jax.ShapeDtypeStruct((TERM_ROWS, width), f32),
        ),
        in_specs=[vmem] * 3,
        out_specs=(vmem,) * 3,
        scratch_shapes=[
            pltpu.VMEM((width // LANES * (frames + 2 * PAD), LANES), f32),
            pltpu.VMEM((width // LANES * (frames + 2 * PAD), LANES), f32),
            pltpu.VMEM((frames, width), f32),
            pltpu.VMEM((width // LANES * (ROWS + PARAM_ROWS), LANES), f32),
            pltpu.VMEM((frames, LANES), f32),
            pltpu.VMEM((frames, LANES), f32),
            pltpu.VMEM((frames, LANES), f32),
            pltpu.VMEM((frames, LANES), f32),
            pltpu.VMEM((32 * ROWS, LANES), f32),
        ],
        compiler_params=pltpu.CompilerParams(vmem_limit_bytes=56 * 1024 * 1024),
    )(frames_in, upstream, params)


def per_device(conv_input, cotangent, kernel, conv_bias, ln_gain, ln_bias):
    taps = kernel.shape[0]
    packed = jnp.concatenate(
        [kernel, jnp.zeros_like(conv_bias)[None], conv_bias[None], ln_gain[None], ln_bias[None]], 0
    )
    packed = jnp.pad(packed, ((0, PARAM_ROWS - packed.shape[0]), (0, 0)))
    gathered = lax.all_gather(packed, "shard", axis=1, tiled=True)
    activated, grad_input, terms = local_part(conv_input[0], cotangent[0], gathered, taps)
    share_sum = lax.psum_scatter(terms, "shard", scatter_dimension=1, tiled=True)
    summed = lax.psum(share_sum, "rep")
    clips = conv_input.shape[0] * lax.axis_size("rep") * lax.axis_size("shard")
    grads = summed * (1.0 / math.sqrt(clips * conv_input.shape[1]))
    return (activated[None], grad_input[None], grads[:taps], grads[taps], grads[taps + 1], grads[taps + 2])


def solution(mesh):
    clips = P(("rep", "shard"), None, None)
    specs = (P(None, "shard"), P("shard"), P("shard"), P("shard"))
    return jax.shard_map(
        per_device, mesh=mesh, in_specs=(clips, clips) + specs, out_specs=(clips, clips) + specs,
        check_vma=False,
    )
```

```python
import math

import jax
import jax.numpy as jnp
from jax import lax
from jax.experimental import pallas as pl
from jax.experimental.pallas import tpu as pltpu
from jax.sharding import PartitionSpec as P

LANES = 128
ROWS = 8
PAD = 16
PARAM_ROWS = 48
TERM_ROWS = 40


def lanes_of(index):
    return pl.ds(pl.multiple_of(index * LANES, LANES), LANES)


def shifted_taps(src, base, coef_ref, coef_row, count):
    def by_phase(phase, totals):
        totals = list(totals)
        coefs = [
            jnp.broadcast_to(coef_ref[pl.ds(coef_row(ROWS * a + phase), 1), :], (ROWS, LANES))
            for a in range(4)
        ]
        for m in range(count + 3):
            value = src[pl.ds(base + ROWS * m + phase + 1, ROWS), :]
            for a in range(4):
                if 0 <= m - a < count:
                    totals[m - a] = totals[m - a] + coefs[a] * value
        return tuple(totals)

    return by_phase


def local_kernel(taps, x_ref, cot_ref, par_ref, act_ref, gin_ref, terms_ref,
                 xp, gp, conv, pf, row_a, row_b, row_c, row_d, acc):
    frames, width = x_ref.shape
    count = frames // ROWS
    tiles = width // LANES
    per = tiles // par_ref.shape[0]
    zeros_tile = jnp.zeros((ROWS, LANES), jnp.float32)

    def rows(i):
        return pl.ds(ROWS * i, ROWS)

    long = frames + 2 * PAD
    held = ROWS + PARAM_ROWS

    def at_long(c, start, size):
        return pl.ds(pl.multiple_of(c * long + start, ROWS), size)

    def at_held(c, start, size):
        return pl.ds(c * held + start, size)

    row_a[...] = jnp.zeros_like(row_a)
    row_c[...] = jnp.zeros_like(row_c)
    row_d[...] = jnp.zeros_like(row_d)

    def forward(c, carry):
        lanes = lanes_of(c)
        pf[at_held(c, 0, ROWS), :] = zeros_tile
        pf[at_held(c, ROWS, PARAM_ROWS), :] = par_ref[c // per, :, lanes_of(c % per)].astype(jnp.float32)
        for ref in (xp, gp):
            for start in (0, PAD + frames):
                ref[at_long(c, start, PAD), :] = jnp.zeros((PAD, LANES), jnp.float32)
        xp[at_long(c, PAD, frames), :] = x_ref[:, lanes].astype(jnp.float32)
        bias = jnp.broadcast_to(pf[at_held(c, ROWS + taps + 1, 1), :], (ROWS, LANES))
        totals = lax.fori_loop(
            0,
            ROWS,
            shifted_taps(xp, c * long, pf, lambda j: c * held + ROWS + j, count),
            (bias,) * count,
        )
        for i in range(count):
            conv[rows(i), lanes] = totals[i]
            row_a[rows(i), :] += totals[i]
        return carry

    lax.fori_loop(0, tiles, forward, 0)

    def stats(i, carry):
        at = pl.ds(pl.multiple_of(i * ROWS, ROWS), ROWS)
        mean = jnp.sum(row_a[at, :], axis=-1, keepdims=True) * (1.0 / width)
        mean = jnp.broadcast_to(mean, (ROWS, LANES))
        parts = [zeros_tile] * 4
        for c in range(tiles):
            off = conv[at, c * LANES : (c + 1) * LANES] - mean
            parts[c % 4] = parts[c % 4] + off * off
        square = (parts[0] + parts[1]) + (parts[2] + parts[3])
        var = jnp.sum(square, axis=-1, keepdims=True) * (1.0 / width)
        row_a[at, :] = mean
        row_b[at, :] = jnp.broadcast_to(lax.rsqrt(var + 1e-05), (ROWS, LANES))
        return carry

    lax.fori_loop(0, count, stats, 0)

    def pointwise(c, carry):
        lanes = lanes_of(c)
        gain = jnp.broadcast_to(pf[at_held(c, ROWS + taps + 2, 1), :], (ROWS, LANES))
        shift = jnp.broadcast_to(pf[at_held(c, ROWS + taps + 3, 1), :], (ROWS, LANES))
        for_gain = [zeros_tile] * 2
        for_bias = [zeros_tile] * 2
        for pair in range(count // 2):
            two = pl.ds(2 * ROWS * pair, 2 * ROWS)
            upstream = cot_ref[two, lanes].astype(jnp.float32)
            acts = []
            for half in range(2):
                i = 2 * pair + half
                normed = (conv[rows(i), lanes] - row_a[rows(i), :]) * row_b[rows(i), :]
                affine = gain * normed + shift
                squash = 0.5 + 0.5 * jnp.tanh(0.5 * affine)
                acts.append(affine * squash)
                up = upstream[half * ROWS : (half + 1) * ROWS]
                grad_affine = up * squash * (1.0 + affine * (1.0 - squash))
                grad_normed = grad_affine * gain
                conv[rows(i), lanes] = normed
                gp[at_long(c, PAD + ROWS * i, ROWS), :] = grad_normed
                row_c[rows(i), :] += grad_normed
                row_d[rows(i), :] += grad_normed * normed
                for_gain[half] = for_gain[half] + grad_affine * normed
                for_bias[half] = for_bias[half] + grad_affine
            act_ref[two, lanes] = jnp.concatenate(acts, 0).astype(jnp.bfloat16)
        terms_ref[c // per, 32:40, lanes_of(c % per)] = zeros_tile
        terms_ref[c // per, 32:33, lanes_of(c % per)] = jnp.sum(for_gain[0] + for_gain[1], axis=0, keepdims=True)
        terms_ref[c // per, 33:34, lanes_of(c % per)] = jnp.sum(for_bias[0] + for_bias[1], axis=0, keepdims=True)
        return carry

    lax.fori_loop(0, tiles, pointwise, 0)

    def means(i, carry):
        at = pl.ds(pl.multiple_of(i * ROWS, ROWS), ROWS)
        for ref in (row_c, row_d):
            mean = jnp.sum(ref[at, :], axis=-1, keepdims=True) * (1.0 / width)
            ref[at, :] = jnp.broadcast_to(mean, (ROWS, LANES))
        return carry

    lax.fori_loop(0, count, means, 0)

    def weights(c, carry):
        lanes = lanes_of(c)
        grads = []
        total = [zeros_tile] * 2
        for i in range(count):
            grad = row_b[rows(i), :] * (
                gp[at_long(c, PAD + ROWS * i, ROWS), :] - row_c[rows(i), :] - conv[rows(i), lanes] * row_d[rows(i), :]
            )
            gp[at_long(c, PAD + ROWS * i, ROWS), :] = grad
            total[i % 2] = total[i % 2] + grad
            grads.append(grad)

        def by_phase(phase, carry):
            sums = [[zeros_tile, zeros_tile] for _ in range(4)]
            for m in range(count + 3):
                value = xp[pl.ds(c * long + ROWS * m + phase + 1, ROWS), :]
                for a in range(4):
                    if 0 <= m - a < count:
                        sums[a][m % 2] = sums[a][m % 2] + grads[m - a] * value
            for a in range(4):
                start = pl.multiple_of((ROWS * a + phase) * ROWS, ROWS)
                acc[pl.ds(start, ROWS), :] = sums[a][0] + sums[a][1]
            return carry

        lax.fori_loop(0, ROWS, by_phase, 0)
        acc[taps * ROWS : (taps + 1) * ROWS, :] = total[0] + total[1]
        summed = acc[pl.ds(0, 32, stride=ROWS), :]
        for s in range(1, ROWS):
            summed = summed + acc[pl.ds(s, 32, stride=ROWS), :]
        terms_ref[c // per, 0:32, lanes_of(c % per)] = summed
        return carry

    lax.fori_loop(0, tiles, weights, 0)

    def inputs(c, carry):
        lanes = lanes_of(c)
        totals = lax.fori_loop(
            0,
            ROWS,
            shifted_taps(gp, c * long, pf, lambda j: c * held + ROWS + taps - 1 - j, count),
            (zeros_tile,) * count,
        )
        for i in range(count // 2):
            both = jnp.concatenate([totals[2 * i], totals[2 * i + 1]], 0)
            gin_ref[pl.ds(2 * ROWS * i, 2 * ROWS), lanes] = both.astype(jnp.bfloat16)
        return carry

    lax.fori_loop(0, tiles, inputs, 0)


def local_part(frames_in, upstream, params, taps):
    frames, width = frames_in.shape
    vmem = pl.BlockSpec(memory_space=pltpu.VMEM)
    f32 = jnp.float32
    return pl.pallas_call(
        lambda *refs: local_kernel(taps, *refs),
        out_shape=(
            jax.ShapeDtypeStruct((frames, width), jnp.bfloat16),
            jax.ShapeDtypeStruct((frames, width), jnp.bfloat16),
            jax.ShapeDtypeStruct((params.shape[0], TERM_ROWS, params.shape[2]), f32),
        ),
        in_specs=[vmem] * 3,
        out_specs=(vmem,) * 3,
        scratch_shapes=[
            pltpu.VMEM((width // LANES * (frames + 2 * PAD), LANES), f32),
            pltpu.VMEM((width // LANES * (frames + 2 * PAD), LANES), f32),
            pltpu.VMEM((frames, width), f32),
            pltpu.VMEM((width // LANES * (ROWS + PARAM_ROWS), LANES), f32),
            pltpu.VMEM((frames, LANES), f32),
            pltpu.VMEM((frames, LANES), f32),
            pltpu.VMEM((frames, LANES), f32),
            pltpu.VMEM((frames, LANES), f32),
            pltpu.VMEM((32 * ROWS, LANES), f32),
        ],
        compiler_params=pltpu.CompilerParams(vmem_limit_bytes=56 * 1024 * 1024),
    )(frames_in, upstream, params)


def greet(axis_sizes):
    barrier = pltpu.get_barrier_semaphore()
    for axis, size in axis_sizes:
        for k in range(1, size):
            peer = lax.rem(lax.axis_index(axis) + k, size)
            pl.semaphore_signal(
                barrier, inc=1, device_id={axis: peer}, device_id_type=pl.DeviceIdType.MESH
            )
    pl.semaphore_wait(barrier, sum(size - 1 for _, size in axis_sizes))


def send(src, dst, sems, k, axis, peer):
    copy = pltpu.make_async_remote_copy(
        src_ref=src,
        dst_ref=dst,
        send_sem=sems[0].at[k - 1],
        recv_sem=sems[1].at[k - 1],
        device_id={axis: peer},
        device_id_type=pl.DeviceIdType.MESH,
    )
    copy.start()
    return copy


def gather_kernel(groups, own_ref, out_ref, held, send_sem, recv_sem):
    me = lax.axis_index("shard")
    greet([("shard", groups)])
    copies = [
        send(own_ref, held.at[k - 1], (send_sem, recv_sem), k, "shard", lax.rem(me + k, groups))
        for k in range(1, groups)
    ]
    out_ref[me] = own_ref[...]
    for k in range(1, groups):
        copies[k - 1].wait()
        out_ref[lax.rem(me + groups - k, groups)] = held[k - 1]


def sum_kernel(groups, replicas, factor, terms_ref, out_ref, held, part, sems_a, sems_b, sems_c, sems_d):
    me = lax.axis_index("shard")
    mine = lax.axis_index("rep")
    greet([("shard", groups), ("rep", replicas)])
    copies = []
    for k in range(1, groups):
        peer = lax.rem(me + k, groups)
        copies.append(send(terms_ref.at[peer], held.at[k - 1], (sems_a, sems_b), k, "shard", peer))
    total = terms_ref[me]
    for k in range(1, groups):
        copies[k - 1].wait()
        total = total + held[k - 1]
    part[mine] = total
    copies = [
        send(part.at[mine], part.at[mine], (sems_c, sems_d), k, "rep", lax.rem(mine + k, replicas))
        for k in range(1, replicas)
    ]
    for copy in copies:
        copy.wait()
    total = part[0]
    for r in range(1, replicas):
        total = total + part[r]
    out_ref[...] = total * factor


def gather(packed, groups):
    vmem = pl.BlockSpec(memory_space=pltpu.VMEM)
    sems = pltpu.SemaphoreType.DMA((groups - 1,))
    return pl.pallas_call(
        lambda *refs: gather_kernel(groups, *refs),
        out_shape=jax.ShapeDtypeStruct((groups,) + packed.shape, packed.dtype),
        in_specs=[vmem],
        out_specs=vmem,
        scratch_shapes=[pltpu.VMEM((groups - 1,) + packed.shape, packed.dtype), sems, sems],
        compiler_params=pltpu.CompilerParams(
            collective_id=0, has_side_effects=True, vmem_limit_bytes=16 * 1024 * 1024
        ),
    )(packed)


def sum_terms(terms, groups, replicas, factor):
    vmem = pl.BlockSpec(memory_space=pltpu.VMEM)
    block = terms.shape[1:]
    dma = pltpu.SemaphoreType.DMA
    return pl.pallas_call(
        lambda *refs: sum_kernel(groups, replicas, factor, *refs),
        out_shape=jax.ShapeDtypeStruct(block, jnp.float32),
        in_specs=[vmem],
        out_specs=vmem,
        scratch_shapes=[
            pltpu.VMEM((groups - 1,) + block, jnp.float32),
            pltpu.VMEM((replicas,) + block, jnp.float32),
            dma((groups - 1,)),
            dma((groups - 1,)),
            dma((replicas - 1,)),
            dma((replicas - 1,)),
        ],
        compiler_params=pltpu.CompilerParams(
            collective_id=1, has_side_effects=True, vmem_limit_bytes=16 * 1024 * 1024
        ),
    )(terms)


def per_device(conv_input, cotangent, kernel, conv_bias, ln_gain, ln_bias):
    taps, chunk = kernel.shape
    groups, replicas = lax.axis_size("shard"), lax.axis_size("rep")
    clips = conv_input.shape[0] * replicas * groups
    factor = 1.0 / math.sqrt(clips * conv_input.shape[1])
    packed = jnp.concatenate(
        [kernel, jnp.zeros_like(conv_bias)[None], conv_bias[None], ln_gain[None], ln_bias[None]], 0
    )
    packed = jnp.pad(packed, ((0, PARAM_ROWS - packed.shape[0]), (0, 0)))
    direct = chunk % LANES == 0
    if direct:
        gathered = gather(packed, groups)
    else:
        gathered = lax.all_gather(packed, "shard", axis=1, tiled=True)[None]
    activated, grad_input, terms = local_part(conv_input[0], cotangent[0], gathered, taps)
    if direct:
        grads = sum_terms(terms, groups, replicas, factor)
    else:
        share_sum = lax.psum_scatter(terms[0], "shard", scatter_dimension=1, tiled=True)
        grads = lax.psum(share_sum, "rep") * factor
    return (activated[None], grad_input[None], grads[:taps], grads[taps], grads[taps + 1], grads[taps + 2])


def solution(mesh):
    clips = P(("rep", "shard"), None, None)
    specs = (P(None, "shard"), P("shard"), P("shard"), P("shard"))
    return jax.shard_map(
        per_device, mesh=mesh, in_specs=(clips, clips) + specs, out_specs=(clips, clips) + specs,
        check_vma=False,
    )
```

```python
import math

import jax
import jax.numpy as jnp
from jax import lax
from jax.experimental import pallas as pl
from jax.experimental.pallas import tpu as pltpu
from jax.sharding import PartitionSpec as P

LANES = 128
ROWS = 8
PAD = 16
PARAM_ROWS = 48
TERM_ROWS = 40


def lanes_of(index):
    return pl.ds(pl.multiple_of(index * LANES, LANES), LANES)


def shifted_taps(src, base, coef_ref, coef_row, count):
    def by_phase(phase, totals):
        totals = list(totals)
        coefs = [
            jnp.broadcast_to(coef_ref[pl.ds(coef_row(ROWS * a + phase), 1), :], (ROWS, LANES))
            for a in range(4)
        ]
        for m in range(count + 3):
            value = src[pl.ds(base + ROWS * m + phase + 1, ROWS), :]
            for a in range(4):
                if 0 <= m - a < count:
                    totals[m - a] = totals[m - a] + coefs[a] * value
        return tuple(totals)

    return by_phase


def local_kernel(taps, x_ref, cot_ref, par_ref, act_ref, gin_ref, terms_ref,
                 xp, gp, conv, pf, row_a, row_b, row_c, row_d, acc):
    frames, width = x_ref.shape
    count = frames // ROWS
    tiles = width // LANES
    per = tiles // par_ref.shape[0]
    zeros_tile = jnp.zeros((ROWS, LANES), jnp.float32)

    def rows(i):
        return pl.ds(ROWS * i, ROWS)

    long = frames + 2 * PAD
    held = ROWS + PARAM_ROWS

    def at_long(c, start, size):
        return pl.ds(pl.multiple_of(c * long + start, ROWS), size)

    def at_held(c, start, size):
        return pl.ds(c * held + start, size)

    row_a[...] = jnp.zeros_like(row_a)
    row_c[...] = jnp.zeros_like(row_c)
    row_d[...] = jnp.zeros_like(row_d)

    def forward(c, carry):
        lanes = lanes_of(c)
        pf[at_held(c, 0, ROWS), :] = zeros_tile
        pf[at_held(c, ROWS, PARAM_ROWS), :] = par_ref[c // per, :, lanes_of(c % per)].astype(jnp.float32)
        for ref in (xp, gp):
            for start in (0, PAD + frames):
                ref[at_long(c, start, PAD), :] = jnp.zeros((PAD, LANES), jnp.float32)
        xp[at_long(c, PAD, frames), :] = x_ref[:, lanes].astype(jnp.float32)
        bias = jnp.broadcast_to(pf[at_held(c, ROWS + taps + 1, 1), :], (ROWS, LANES))
        totals = lax.fori_loop(
            0,
            ROWS,
            shifted_taps(xp, c * long, pf, lambda j: c * held + ROWS + j, count),
            (bias,) * count,
            unroll=True,
        )
        for i in range(count):
            conv[rows(i), lanes] = totals[i]
            row_a[rows(i), :] += totals[i]
        return carry

    lax.fori_loop(0, tiles, forward, 0)

    def stats(i, carry):
        at = pl.ds(pl.multiple_of(i * ROWS, ROWS), ROWS)
        mean = jnp.sum(row_a[at, :], axis=-1, keepdims=True) * (1.0 / width)
        mean = jnp.broadcast_to(mean, (ROWS, LANES))
        parts = [zeros_tile] * 4
        for c in range(tiles):
            off = conv[at, c * LANES : (c + 1) * LANES] - mean
            parts[c % 4] = parts[c % 4] + off * off
        square = (parts[0] + parts[1]) + (parts[2] + parts[3])
        var = jnp.sum(square, axis=-1, keepdims=True) * (1.0 / width)
        row_a[at, :] = mean
        row_b[at, :] = jnp.broadcast_to(lax.rsqrt(var + 1e-05), (ROWS, LANES))
        return carry

    lax.fori_loop(0, count, stats, 0)

    def pointwise(c, carry):
        lanes = lanes_of(c)
        gain = jnp.broadcast_to(pf[at_held(c, ROWS + taps + 2, 1), :], (ROWS, LANES))
        shift = jnp.broadcast_to(pf[at_held(c, ROWS + taps + 3, 1), :], (ROWS, LANES))
        for_gain = [zeros_tile] * 2
        for_bias = [zeros_tile] * 2
        for pair in range(count // 2):
            two = pl.ds(2 * ROWS * pair, 2 * ROWS)
            upstream = cot_ref[two, lanes].astype(jnp.float32)
            acts = []
            for half in range(2):
                i = 2 * pair + half
                normed = (conv[rows(i), lanes] - row_a[rows(i), :]) * row_b[rows(i), :]
                affine = gain * normed + shift
                squash = 0.5 + 0.5 * jnp.tanh(0.5 * affine)
                acts.append(affine * squash)
                up = upstream[half * ROWS : (half + 1) * ROWS]
                grad_affine = up * squash * (1.0 + affine * (1.0 - squash))
                grad_normed = grad_affine * gain
                conv[rows(i), lanes] = normed
                gp[at_long(c, PAD + ROWS * i, ROWS), :] = grad_normed
                row_c[rows(i), :] += grad_normed
                row_d[rows(i), :] += grad_normed * normed
                for_gain[half] = for_gain[half] + grad_affine * normed
                for_bias[half] = for_bias[half] + grad_affine
            act_ref[two, lanes] = jnp.concatenate(acts, 0).astype(jnp.bfloat16)
        terms_ref[c // per, 32:40, lanes_of(c % per)] = zeros_tile
        terms_ref[c // per, 32:33, lanes_of(c % per)] = jnp.sum(for_gain[0] + for_gain[1], axis=0, keepdims=True)
        terms_ref[c // per, 33:34, lanes_of(c % per)] = jnp.sum(for_bias[0] + for_bias[1], axis=0, keepdims=True)
        return carry

    lax.fori_loop(0, tiles, pointwise, 0)

    def means(i, carry):
        at = pl.ds(pl.multiple_of(i * ROWS, ROWS), ROWS)
        for ref in (row_c, row_d):
            mean = jnp.sum(ref[at, :], axis=-1, keepdims=True) * (1.0 / width)
            ref[at, :] = jnp.broadcast_to(mean, (ROWS, LANES))
        return carry

    lax.fori_loop(0, count, means, 0)

    def weights(c, carry):
        lanes = lanes_of(c)
        grads = []
        total = [zeros_tile] * 2
        for i in range(count):
            grad = row_b[rows(i), :] * (
                gp[at_long(c, PAD + ROWS * i, ROWS), :] - row_c[rows(i), :] - conv[rows(i), lanes] * row_d[rows(i), :]
            )
            gp[at_long(c, PAD + ROWS * i, ROWS), :] = grad
            total[i % 2] = total[i % 2] + grad
            grads.append(grad)

        def by_phase(phase, carry):
            sums = [[zeros_tile, zeros_tile] for _ in range(4)]
            for m in range(count + 3):
                value = xp[pl.ds(c * long + ROWS * m + phase + 1, ROWS), :]
                for a in range(4):
                    if 0 <= m - a < count:
                        sums[a][m % 2] = sums[a][m % 2] + grads[m - a] * value
            for a in range(4):
                start = pl.multiple_of((ROWS * a + phase) * ROWS, ROWS)
                acc[pl.ds(start, ROWS), :] = sums[a][0] + sums[a][1]
            return carry

        lax.fori_loop(0, ROWS, by_phase, 0, unroll=True)
        acc[taps * ROWS : (taps + 1) * ROWS, :] = total[0] + total[1]
        summed = acc[pl.ds(0, 32, stride=ROWS), :]
        for s in range(1, ROWS):
            summed = summed + acc[pl.ds(s, 32, stride=ROWS), :]
        terms_ref[c // per, 0:32, lanes_of(c % per)] = summed
        return carry

    lax.fori_loop(0, tiles, weights, 0)

    def inputs(c, carry):
        lanes = lanes_of(c)
        totals = lax.fori_loop(
            0,
            ROWS,
            shifted_taps(gp, c * long, pf, lambda j: c * held + ROWS + taps - 1 - j, count),
            (zeros_tile,) * count,
            unroll=True,
        )
        for i in range(count // 2):
            both = jnp.concatenate([totals[2 * i], totals[2 * i + 1]], 0)
            gin_ref[pl.ds(2 * ROWS * i, 2 * ROWS), lanes] = both.astype(jnp.bfloat16)
        return carry

    lax.fori_loop(0, tiles, inputs, 0)


def local_part(frames_in, upstream, params, taps):
    frames, width = frames_in.shape
    vmem = pl.BlockSpec(memory_space=pltpu.VMEM)
    f32 = jnp.float32
    return pl.pallas_call(
        lambda *refs: local_kernel(taps, *refs),
        out_shape=(
            jax.ShapeDtypeStruct((frames, width), jnp.bfloat16),
            jax.ShapeDtypeStruct((frames, width), jnp.bfloat16),
            jax.ShapeDtypeStruct((params.shape[0], TERM_ROWS, params.shape[2]), f32),
        ),
        in_specs=[vmem] * 3,
        out_specs=(vmem,) * 3,
        scratch_shapes=[
            pltpu.VMEM((width // LANES * (frames + 2 * PAD), LANES), f32),
            pltpu.VMEM((width // LANES * (frames + 2 * PAD), LANES), f32),
            pltpu.VMEM((frames, width), f32),
            pltpu.VMEM((width // LANES * (ROWS + PARAM_ROWS), LANES), f32),
            pltpu.VMEM((frames, LANES), f32),
            pltpu.VMEM((frames, LANES), f32),
            pltpu.VMEM((frames, LANES), f32),
            pltpu.VMEM((frames, LANES), f32),
            pltpu.VMEM((32 * ROWS, LANES), f32),
        ],
        compiler_params=pltpu.CompilerParams(vmem_limit_bytes=56 * 1024 * 1024),
    )(frames_in, upstream, params)


def greet(axis_sizes):
    barrier = pltpu.get_barrier_semaphore()
    for axis, size in axis_sizes:
        for k in range(1, size):
            peer = lax.rem(lax.axis_index(axis) + k, size)
            pl.semaphore_signal(
                barrier, inc=1, device_id={axis: peer}, device_id_type=pl.DeviceIdType.MESH
            )
    pl.semaphore_wait(barrier, sum(size - 1 for _, size in axis_sizes))


def send(src, dst, sems, k, axis, peer):
    copy = pltpu.make_async_remote_copy(
        src_ref=src,
        dst_ref=dst,
        send_sem=sems[0].at[k - 1],
        recv_sem=sems[1].at[k - 1],
        device_id={axis: peer},
        device_id_type=pl.DeviceIdType.MESH,
    )
    copy.start()
    return copy


def gather_kernel(groups, own_ref, out_ref, held, send_sem, recv_sem):
    me = lax.axis_index("shard")
    greet([("shard", groups)])
    copies = [
        send(own_ref, held.at[k - 1], (send_sem, recv_sem), k, "shard", lax.rem(me + k, groups))
        for k in range(1, groups)
    ]
    out_ref[me] = own_ref[...]
    for k in range(1, groups):
        copies[k - 1].wait()
        out_ref[lax.rem(me + groups - k, groups)] = held[k - 1]


def sum_kernel(groups, replicas, factor, terms_ref, out_ref, held, part, sems_a, sems_b, sems_c, sems_d):
    me = lax.axis_index("shard")
    mine = lax.axis_index("rep")
    greet([("shard", groups), ("rep", replicas)])
    copies = []
    for k in range(1, groups):
        peer = lax.rem(me + k, groups)
        copies.append(send(terms_ref.at[peer], held.at[k - 1], (sems_a, sems_b), k, "shard", peer))
    total = terms_ref[me]
    for k in range(1, groups):
        copies[k - 1].wait()
        total = total + held[k - 1]
    part[mine] = total
    copies = [
        send(part.at[mine], part.at[mine], (sems_c, sems_d), k, "rep", lax.rem(mine + k, replicas))
        for k in range(1, replicas)
    ]
    for copy in copies:
        copy.wait()
    total = part[0]
    for r in range(1, replicas):
        total = total + part[r]
    out_ref[...] = total * factor


def gather(packed, groups):
    vmem = pl.BlockSpec(memory_space=pltpu.VMEM)
    sems = pltpu.SemaphoreType.DMA((groups - 1,))
    return pl.pallas_call(
        lambda *refs: gather_kernel(groups, *refs),
        out_shape=jax.ShapeDtypeStruct((groups,) + packed.shape, packed.dtype),
        in_specs=[vmem],
        out_specs=vmem,
        scratch_shapes=[pltpu.VMEM((groups - 1,) + packed.shape, packed.dtype), sems, sems],
        compiler_params=pltpu.CompilerParams(
            collective_id=0, has_side_effects=True, vmem_limit_bytes=16 * 1024 * 1024
        ),
    )(packed)


def sum_terms(terms, groups, replicas, factor):
    vmem = pl.BlockSpec(memory_space=pltpu.VMEM)
    block = terms.shape[1:]
    dma = pltpu.SemaphoreType.DMA
    return pl.pallas_call(
        lambda *refs: sum_kernel(groups, replicas, factor, *refs),
        out_shape=jax.ShapeDtypeStruct(block, jnp.float32),
        in_specs=[vmem],
        out_specs=vmem,
        scratch_shapes=[
            pltpu.VMEM((groups - 1,) + block, jnp.float32),
            pltpu.VMEM((replicas,) + block, jnp.float32),
            dma((groups - 1,)),
            dma((groups - 1,)),
            dma((replicas - 1,)),
            dma((replicas - 1,)),
        ],
        compiler_params=pltpu.CompilerParams(
            collective_id=1, has_side_effects=True, vmem_limit_bytes=16 * 1024 * 1024
        ),
    )(terms)


def per_device(conv_input, cotangent, kernel, conv_bias, ln_gain, ln_bias):
    taps, chunk = kernel.shape
    groups, replicas = lax.axis_size("shard"), lax.axis_size("rep")
    clips = conv_input.shape[0] * replicas * groups
    factor = 1.0 / math.sqrt(clips * conv_input.shape[1])
    packed = jnp.concatenate(
        [kernel, jnp.zeros_like(conv_bias)[None], conv_bias[None], ln_gain[None], ln_bias[None]], 0
    )
    packed = jnp.pad(packed, ((0, PARAM_ROWS - packed.shape[0]), (0, 0)))
    direct = chunk % LANES == 0
    if direct:
        gathered = gather(packed, groups)
    else:
        gathered = lax.all_gather(packed, "shard", axis=1, tiled=True)[None]
    activated, grad_input, terms = local_part(conv_input[0], cotangent[0], gathered, taps)
    if direct:
        grads = sum_terms(terms, groups, replicas, factor)
    else:
        share_sum = lax.psum_scatter(terms[0], "shard", scatter_dimension=1, tiled=True)
        grads = lax.psum(share_sum, "rep") * factor
    return (activated[None], grad_input[None], grads[:taps], grads[taps], grads[taps + 1], grads[taps + 2])


def solution(mesh):
    clips = P(("rep", "shard"), None, None)
    specs = (P(None, "shard"), P("shard"), P("shard"), P("shard"))
    return jax.shard_map(
        per_device, mesh=mesh, in_specs=(clips, clips) + specs, out_specs=(clips, clips) + specs,
        check_vma=False,
    )
```

```python
import math

import jax
import jax.numpy as jnp
from jax import lax
from jax.experimental import pallas as pl
from jax.experimental.pallas import tpu as pltpu
from jax.sharding import PartitionSpec as P

LANES = 128
ROWS = 8
PAD = 16
PARAM_ROWS = 48
TERM_ROWS = 40


def lanes_of(index):
    return pl.ds(pl.multiple_of(index * LANES, LANES), LANES)


def shifted_taps(src, base, coef_ref, coef_row, count):
    def by_phase(phase, totals):
        totals = list(totals)
        coefs = [
            jnp.broadcast_to(coef_ref[pl.ds(coef_row(ROWS * a + phase), 1), :], (ROWS, LANES))
            for a in range(4)
        ]
        for m in range(count + 3):
            value = src[pl.ds(base + ROWS * m + phase + 1, ROWS), :]
            for a in range(4):
                if 0 <= m - a < count:
                    totals[m - a] = totals[m - a] + coefs[a] * value
        return tuple(totals)

    return by_phase


def local_kernel(taps, x_ref, cot_ref, par_ref, act_ref, gin_ref, terms_ref,
                 xp, gp, conv, pf, row_a, row_b, row_c, row_d, acc):
    frames, width = x_ref.shape
    count = frames // ROWS
    tiles = width // LANES
    per = tiles // par_ref.shape[0]
    zeros_tile = jnp.zeros((ROWS, LANES), jnp.float32)

    def rows(i):
        return pl.ds(ROWS * i, ROWS)

    long = frames + 2 * PAD
    held = ROWS + PARAM_ROWS

    def at_long(c, start, size):
        return pl.ds(pl.multiple_of(c * long + start, ROWS), size)

    def at_held(c, start, size):
        return pl.ds(c * held + start, size)

    row_a[...] = jnp.zeros_like(row_a)
    row_c[...] = jnp.zeros_like(row_c)
    row_d[...] = jnp.zeros_like(row_d)

    def forward(c, carry):
        lanes = lanes_of(c)
        pf[at_held(c, 0, ROWS), :] = zeros_tile
        pf[at_held(c, ROWS, PARAM_ROWS), :] = par_ref[c // per, :, lanes_of(c % per)].astype(jnp.float32)
        for ref in (xp, gp):
            for start in (0, PAD + frames):
                ref[at_long(c, start, PAD), :] = jnp.zeros((PAD, LANES), jnp.float32)
        xp[at_long(c, PAD, frames), :] = x_ref[:, lanes].astype(jnp.float32)
        bias = jnp.broadcast_to(pf[at_held(c, ROWS + taps + 1, 1), :], (ROWS, LANES))
        totals = lax.fori_loop(
            0,
            ROWS,
            shifted_taps(xp, c * long, pf, lambda j: c * held + ROWS + j, count),
            (bias,) * count,
            unroll=True,
        )
        for i in range(count):
            conv[rows(i), lanes] = totals[i]
            row_a[rows(i), :] += totals[i]
        return carry

    lax.fori_loop(0, tiles, forward, 0)

    def stats(i, carry):
        at = pl.ds(pl.multiple_of(i * ROWS, ROWS), ROWS)
        mean = jnp.sum(row_a[at, :], axis=-1, keepdims=True) * (1.0 / width)
        mean = jnp.broadcast_to(mean, (ROWS, LANES))
        parts = [zeros_tile] * 4
        for c in range(tiles):
            off = conv[at, c * LANES : (c + 1) * LANES] - mean
            parts[c % 4] = parts[c % 4] + off * off
        square = (parts[0] + parts[1]) + (parts[2] + parts[3])
        var = jnp.sum(square, axis=-1, keepdims=True) * (1.0 / width)
        row_a[at, :] = mean
        row_b[at, :] = jnp.broadcast_to(lax.rsqrt(var + 1e-05), (ROWS, LANES))
        return carry

    lax.fori_loop(0, count, stats, 0, unroll=4)

    def pointwise(c, carry):
        lanes = lanes_of(c)
        gain = jnp.broadcast_to(pf[at_held(c, ROWS + taps + 2, 1), :], (ROWS, LANES))
        shift = jnp.broadcast_to(pf[at_held(c, ROWS + taps + 3, 1), :], (ROWS, LANES))
        for_gain = [zeros_tile] * 2
        for_bias = [zeros_tile] * 2
        for pair in range(count // 2):
            two = pl.ds(2 * ROWS * pair, 2 * ROWS)
            upstream = cot_ref[two, lanes].astype(jnp.float32)
            acts = []
            for half in range(2):
                i = 2 * pair + half
                normed = (conv[rows(i), lanes] - row_a[rows(i), :]) * row_b[rows(i), :]
                affine = gain * normed + shift
                squash = 0.5 + 0.5 * jnp.tanh(0.5 * affine)
                acts.append(affine * squash)
                up = upstream[half * ROWS : (half + 1) * ROWS]
                grad_affine = up * squash * (1.0 + affine * (1.0 - squash))
                grad_normed = grad_affine * gain
                conv[rows(i), lanes] = normed
                gp[at_long(c, PAD + ROWS * i, ROWS), :] = grad_normed
                row_c[rows(i), :] += grad_normed
                row_d[rows(i), :] += grad_normed * normed
                for_gain[half] = for_gain[half] + grad_affine * normed
                for_bias[half] = for_bias[half] + grad_affine
            act_ref[two, lanes] = jnp.concatenate(acts, 0).astype(jnp.bfloat16)
        terms_ref[c // per, 32:40, lanes_of(c % per)] = zeros_tile
        terms_ref[c // per, 32:33, lanes_of(c % per)] = jnp.sum(for_gain[0] + for_gain[1], axis=0, keepdims=True)
        terms_ref[c // per, 33:34, lanes_of(c % per)] = jnp.sum(for_bias[0] + for_bias[1], axis=0, keepdims=True)
        return carry

    lax.fori_loop(0, tiles, pointwise, 0)

    def means(i, carry):
        at = pl.ds(pl.multiple_of(i * ROWS, ROWS), ROWS)
        for ref in (row_c, row_d):
            mean = jnp.sum(ref[at, :], axis=-1, keepdims=True) * (1.0 / width)
            ref[at, :] = jnp.broadcast_to(mean, (ROWS, LANES))
        return carry

    lax.fori_loop(0, count, means, 0, unroll=8)

    def weights(c, carry):
        lanes = lanes_of(c)
        grads = []
        total = [zeros_tile] * 2
        for i in range(count):
            grad = row_b[rows(i), :] * (
                gp[at_long(c, PAD + ROWS * i, ROWS), :] - row_c[rows(i), :] - conv[rows(i), lanes] * row_d[rows(i), :]
            )
            gp[at_long(c, PAD + ROWS * i, ROWS), :] = grad
            total[i % 2] = total[i % 2] + grad
            grads.append(grad)

        def by_phase(phase, carry):
            sums = [[zeros_tile, zeros_tile] for _ in range(4)]
            for m in range(count + 3):
                value = xp[pl.ds(c * long + ROWS * m + phase + 1, ROWS), :]
                for a in range(4):
                    if 0 <= m - a < count:
                        sums[a][m % 2] = sums[a][m % 2] + grads[m - a] * value
            for a in range(4):
                start = pl.multiple_of((ROWS * a + phase) * ROWS, ROWS)
                acc[pl.ds(start, ROWS), :] = sums[a][0] + sums[a][1]
            return carry

        lax.fori_loop(0, ROWS, by_phase, 0, unroll=True)
        acc[taps * ROWS : (taps + 1) * ROWS, :] = total[0] + total[1]
        summed = acc[pl.ds(0, 32, stride=ROWS), :]
        for s in range(1, ROWS):
            summed = summed + acc[pl.ds(s, 32, stride=ROWS), :]
        terms_ref[c // per, 0:32, lanes_of(c % per)] = summed
        return carry

    lax.fori_loop(0, tiles, weights, 0)

    def inputs(c, carry):
        lanes = lanes_of(c)
        totals = lax.fori_loop(
            0,
            ROWS,
            shifted_taps(gp, c * long, pf, lambda j: c * held + ROWS + taps - 1 - j, count),
            (zeros_tile,) * count,
            unroll=True,
        )
        for i in range(count // 2):
            both = jnp.concatenate([totals[2 * i], totals[2 * i + 1]], 0)
            gin_ref[pl.ds(2 * ROWS * i, 2 * ROWS), lanes] = both.astype(jnp.bfloat16)
        return carry

    lax.fori_loop(0, tiles, inputs, 0)


def local_part(frames_in, upstream, params, taps):
    frames, width = frames_in.shape
    vmem = pl.BlockSpec(memory_space=pltpu.VMEM)
    f32 = jnp.float32
    return pl.pallas_call(
        lambda *refs: local_kernel(taps, *refs),
        out_shape=(
            jax.ShapeDtypeStruct((frames, width), jnp.bfloat16),
            jax.ShapeDtypeStruct((frames, width), jnp.bfloat16),
            jax.ShapeDtypeStruct((params.shape[0], TERM_ROWS, params.shape[2]), f32),
        ),
        in_specs=[vmem] * 3,
        out_specs=(vmem,) * 3,
        scratch_shapes=[
            pltpu.VMEM((width // LANES * (frames + 2 * PAD), LANES), f32),
            pltpu.VMEM((width // LANES * (frames + 2 * PAD), LANES), f32),
            pltpu.VMEM((frames, width), f32),
            pltpu.VMEM((width // LANES * (ROWS + PARAM_ROWS), LANES), f32),
            pltpu.VMEM((frames, LANES), f32),
            pltpu.VMEM((frames, LANES), f32),
            pltpu.VMEM((frames, LANES), f32),
            pltpu.VMEM((frames, LANES), f32),
            pltpu.VMEM((32 * ROWS, LANES), f32),
        ],
        compiler_params=pltpu.CompilerParams(vmem_limit_bytes=56 * 1024 * 1024),
    )(frames_in, upstream, params)


def greet(axis_sizes):
    barrier = pltpu.get_barrier_semaphore()
    for axis, size in axis_sizes:
        for k in range(1, size):
            peer = lax.rem(lax.axis_index(axis) + k, size)
            pl.semaphore_signal(
                barrier, inc=1, device_id={axis: peer}, device_id_type=pl.DeviceIdType.MESH
            )
    pl.semaphore_wait(barrier, sum(size - 1 for _, size in axis_sizes))


def send(src, dst, sems, k, axis, peer):
    copy = pltpu.make_async_remote_copy(
        src_ref=src,
        dst_ref=dst,
        send_sem=sems[0].at[k - 1],
        recv_sem=sems[1].at[k - 1],
        device_id={axis: peer},
        device_id_type=pl.DeviceIdType.MESH,
    )
    copy.start()
    return copy


def gather_kernel(groups, own_ref, out_ref, held, send_sem, recv_sem):
    me = lax.axis_index("shard")
    greet([("shard", groups)])
    copies = [
        send(own_ref, held.at[k - 1], (send_sem, recv_sem), k, "shard", lax.rem(me + k, groups))
        for k in range(1, groups)
    ]
    out_ref[me] = own_ref[...]
    for k in range(1, groups):
        copies[k - 1].wait()
        out_ref[lax.rem(me + groups - k, groups)] = held[k - 1]


def sum_kernel(groups, replicas, factor, terms_ref, out_ref, held, part, sems_a, sems_b, sems_c, sems_d):
    me = lax.axis_index("shard")
    mine = lax.axis_index("rep")
    greet([("shard", groups), ("rep", replicas)])
    copies = []
    for k in range(1, groups):
        peer = lax.rem(me + k, groups)
        copies.append(send(terms_ref.at[peer], held.at[k - 1], (sems_a, sems_b), k, "shard", peer))
    total = terms_ref[me]
    for k in range(1, groups):
        copies[k - 1].wait()
        total = total + held[k - 1]
    part[mine] = total
    copies = [
        send(part.at[mine], part.at[mine], (sems_c, sems_d), k, "rep", lax.rem(mine + k, replicas))
        for k in range(1, replicas)
    ]
    for copy in copies:
        copy.wait()
    total = part[0]
    for r in range(1, replicas):
        total = total + part[r]
    out_ref[...] = total * factor


def gather(packed, groups):
    vmem = pl.BlockSpec(memory_space=pltpu.VMEM)
    sems = pltpu.SemaphoreType.DMA((groups - 1,))
    return pl.pallas_call(
        lambda *refs: gather_kernel(groups, *refs),
        out_shape=jax.ShapeDtypeStruct((groups,) + packed.shape, packed.dtype),
        in_specs=[vmem],
        out_specs=vmem,
        scratch_shapes=[pltpu.VMEM((groups - 1,) + packed.shape, packed.dtype), sems, sems],
        compiler_params=pltpu.CompilerParams(
            collective_id=0, has_side_effects=True, vmem_limit_bytes=16 * 1024 * 1024
        ),
    )(packed)


def sum_terms(terms, groups, replicas, factor):
    vmem = pl.BlockSpec(memory_space=pltpu.VMEM)
    block = terms.shape[1:]
    dma = pltpu.SemaphoreType.DMA
    return pl.pallas_call(
        lambda *refs: sum_kernel(groups, replicas, factor, *refs),
        out_shape=jax.ShapeDtypeStruct(block, jnp.float32),
        in_specs=[vmem],
        out_specs=vmem,
        scratch_shapes=[
            pltpu.VMEM((groups - 1,) + block, jnp.float32),
            pltpu.VMEM((replicas,) + block, jnp.float32),
            dma((groups - 1,)),
            dma((groups - 1,)),
            dma((replicas - 1,)),
            dma((replicas - 1,)),
        ],
        compiler_params=pltpu.CompilerParams(
            collective_id=1, has_side_effects=True, vmem_limit_bytes=16 * 1024 * 1024
        ),
    )(terms)


def per_device(conv_input, cotangent, kernel, conv_bias, ln_gain, ln_bias):
    taps, chunk = kernel.shape
    groups, replicas = lax.axis_size("shard"), lax.axis_size("rep")
    clips = conv_input.shape[0] * replicas * groups
    factor = 1.0 / math.sqrt(clips * conv_input.shape[1])
    packed = jnp.concatenate(
        [kernel, jnp.zeros_like(conv_bias)[None], conv_bias[None], ln_gain[None], ln_bias[None]], 0
    )
    packed = jnp.pad(packed, ((0, PARAM_ROWS - packed.shape[0]), (0, 0)))
    direct = chunk % LANES == 0
    if direct:
        gathered = gather(packed, groups)
    else:
        gathered = lax.all_gather(packed, "shard", axis=1, tiled=True)[None]
    activated, grad_input, terms = local_part(conv_input[0], cotangent[0], gathered, taps)
    if direct:
        grads = sum_terms(terms, groups, replicas, factor)
    else:
        share_sum = lax.psum_scatter(terms[0], "shard", scatter_dimension=1, tiled=True)
        grads = lax.psum(share_sum, "rep") * factor
    return (activated[None], grad_input[None], grads[:taps], grads[taps], grads[taps + 1], grads[taps + 2])


def solution(mesh):
    clips = P(("rep", "shard"), None, None)
    specs = (P(None, "shard"), P("shard"), P("shard"), P("shard"))
    return jax.shard_map(
        per_device, mesh=mesh, in_specs=(clips, clips) + specs, out_specs=(clips, clips) + specs,
        check_vma=False,
    )
```
